32 devices in a mesh: row: 8 (over z, y), col: 4 (over x, core).
Axes of the slice: x: 2, y: 2, z: 4, core: 2. Of those that a mesh axis runs over, the one named last changes fastest.
Arguments:
- features: bfloat16 [256, 32768], P('col', 'row'), may hold values from -6 to 6
- weight: bfloat16 [256, 256], replicated, may hold values from -0.375 to 0.375
- cotangent: bfloat16 [256, 32768], P('col', 'row'), may hold values from -6 to 6
- degree: int32 [32768], P('row'), may hold values from 8 to 256
- tile_src: int32 [256, 10], P('row'), may hold values from 0 to 255, as said below
- tile_count: int32 [256], P('row'), may hold values from 1 to 10, as said below
- tile_vals: bfloat16 [256, 10, 128, 128], P('row'), may hold values from -18 to 18
Outputs:
- output: bfloat16 [256, 32768], P('col', 'row')
- input_grad: float32 [256, 32768], P('col', 'row')
- weight_grad: float32 [256, 256], P(None, 'col')
The draws below stay inside these ranges and needn't reach their ends.
Inputs may be any that keep to these rules, and one draw needn't show every extreme that they name: `tile_src`: slot 0 of every destination block names the block itself. Its other slots name distinct blocks other than itself, each held by the same index of row as the destination block or by one of the two next to it. `tile_count`: slots at or past this count are empty: their tile_src and tile_vals entries take no part. Every index of row holds a block with all 10 slots live.
All inputs are finite; a program needn't handle non-finite values.
Results may differ from the reference program's by a relative error of at most 0.0057.
Values may be sent and summed in bfloat16 or wider, within the bound.
No kernel may reach another device: no remote copies, remote signals or barrier semaphores. Data moves between devices by JAX's collectives and lax.ppermute only.
A program may use at most 64 MiB of HBM per device.

```python
import math
import jax
import jax.numpy as jnp
from jax import lax

D = 256
TILE = 128
TPB = 10
BLOCKS_ROW = 32
NBLK = 256
NODES = 32768
N_ROW = 8


def draw_tile_src(key, part):
    key = jax.random.fold_in(key, 11)
    total = BLOCKS_ROW * N_ROW
    block_ids = jnp.arange(total, dtype=jnp.int32)
    owner_row = block_ids // BLOCKS_ROW
    candidate = jnp.arange(3 * BLOCKS_ROW, dtype=jnp.int32)
    global_ids = (owner_row[:, None] - 1) * BLOCKS_ROW + candidate[None, :]
    excluded = (global_ids < 0) | (global_ids >= total) | (global_ids == block_ids[:, None])
    scores = jax.random.randint(key, (total, 3 * BLOCKS_ROW), 0, 1 << 20, dtype=jnp.int32)
    scores = jnp.where(excluded, 1 << 21, scores) * (3 * BLOCKS_ROW) + candidate[None, :]
    ranking = jnp.argsort(scores, axis=1, stable=True)[:, :TPB - 1]
    picked = jnp.take_along_axis(global_ids, ranking, axis=1)
    return jnp.concatenate([block_ids[:, None], picked], axis=1).astype(jnp.int32)


def draw_tile_count(key, part):
    key = jax.random.fold_in(key, 23)
    key_level, key_drawn, key_forced = jax.random.split(key, 3)
    load_level = jax.random.randint(key_level, (N_ROW,), 1, 5, dtype=jnp.int32)
    upper = jnp.maximum(2, load_level * TPB // 4 + 1)
    drawn = jax.random.randint(key_drawn, (N_ROW, BLOCKS_ROW), 1, upper[:, None], dtype=jnp.int32)
    forced = jax.random.randint(key_forced, (N_ROW,), 0, BLOCKS_ROW, dtype=jnp.int32)
    position = jnp.arange(BLOCKS_ROW, dtype=jnp.int32)
    counts = jnp.where(position[None, :] == forced[:, None], TPB, jnp.minimum(drawn, TPB))
    return counts.reshape(-1).astype(jnp.int32)


def with_ends(array, key, smallest, high):
    dims = array.shape
    index_at = [jax.random.randint(jax.random.fold_in(key, axis), (), 0, dims[axis]) for axis in range(len(dims))]
    array = array.at[tuple(index_at)].set(smallest)
    longest = dims.index(max(dims))
    index_at[longest] = (index_at[longest] + 1) % dims[longest]
    return array.at[tuple(index_at)].set(high)


def level_of(stream_key, extent, shards, low, top_value):
    def one(axis_at, shards_of):
        steps = jax.random.uniform(jax.random.fold_in(jax.random.fold_in(stream_key, 6), axis_at), (shards_of,), jnp.float32, low / len(shards), top_value / len(shards))
        return jnp.repeat(jnp.exp(steps), extent[axis_at] // shards_of).reshape((-1,) + (1,) * (len(extent) - axis_at - 1))

    level = one(*shards[0])
    for cut in shards[1:]:
        level = level * one(*cut)
    return level


def normal_values(key, extent, width, bound, pieces=(), kind=jnp.bfloat16):
    values = width * jax.random.normal(key, extent, jnp.float32)
    if pieces:
        values = values * level_of(key, extent, pieces, -0.22, 0.18)
    return jnp.clip(values, -bound, bound).astype(kind)


def setup_inputs(seed: int = 0) -> dict:
    arg_keys = jax.random.split(jax.random.key(seed), 8)
    return {
        "features": normal_values(arg_keys[0], (D, NODES), 1.0, 6.0, ((0, 4), (1, 8))),
        "weight": normal_values(arg_keys[1], (D, D), D ** -0.5, 0.375),
        "cotangent": normal_values(arg_keys[2], (D, NODES), 1.0, 6.0, ((0, 4), (1, 8))),
        "degree": with_ends(jax.random.randint(arg_keys[3], (NODES,), 8, 257), jax.random.fold_in(arg_keys[3], 1), 8, 256).astype(jnp.int32),
        "tile_src": draw_tile_src(jax.random.fold_in(arg_keys[7], 71), 0),
        "tile_count": draw_tile_count(jax.random.fold_in(arg_keys[7], 71), 0),
        "tile_vals": normal_values(arg_keys[6], (NBLK, TPB, TILE, TILE), 3.0, 18.0, ((0, 8),)),
    }


def aggregate(feats, tile_src, tile_count, tile_vals):
    by_block = feats.reshape(feats.shape[0], NBLK, TILE)
    slot_ids = jnp.arange(TPB, dtype=jnp.int32)

    def per_group(group_args):
        source_ids, live_count, tile_block = group_args
        live_mask = (slot_ids[None, :] < live_count[:, None]).astype(jnp.float32)
        sources = by_block[:, source_ids] * live_mask[None, :, :, None]
        return jnp.einsum('fbtk,btjk->fbj', sources, tile_block.astype(jnp.float32), precision=lax.Precision.HIGHEST)
    grouped = lax.map(per_group, (tile_src.reshape(N_ROW, BLOCKS_ROW, TPB), tile_count.reshape(N_ROW, BLOCKS_ROW), tile_vals.reshape(N_ROW, BLOCKS_ROW, TPB, TILE, TILE)))
    return jnp.moveaxis(grouped, 0, 1).reshape(feats.shape[0], NODES)

def reference(features, weight, cotangent, degree, tile_src, tile_count, tile_vals):
    inv_root = lax.rsqrt(degree.astype(jnp.float32))
    scaled = (features.astype(jnp.float32) * inv_root[None, :]).astype(jnp.bfloat16)

    def linear(feats):
        return aggregate(feats, tile_src, tile_count, tile_vals)
    summed, pullback = jax.vjp(linear, scaled.astype(jnp.float32))
    aggregated = (summed * inv_root[None, :]).astype(jnp.bfloat16)
    output = jnp.dot(weight.T, aggregated, preferred_element_type=jnp.float32).astype(jnp.bfloat16)
    weight_grad = jnp.dot(aggregated, cotangent.T, preferred_element_type=jnp.float32) / math.sqrt(NODES)
    grad_full = jnp.dot(weight, cotangent, preferred_element_type=jnp.float32)
    grad_scaled = (grad_full * inv_root[None, :]).astype(jnp.bfloat16)
    back_sum = pullback(grad_scaled.astype(jnp.float32))[0]
    input_grad = back_sum * inv_root[None, :]
    return (output, input_grad, weight_grad)
```

```python
import functools
import math

import jax
import jax.numpy as jnp
from jax import lax
from jax.experimental import pallas as pl
from jax.experimental.pallas import tpu as pltpu
from jax.sharding import PartitionSpec as P

CONTRACT_LAST = (((1,), (1,)), ((), ()))
VMEM_BYTES = 40 * 1024 * 1024


def xor_pairs(count, bit):
    return [(i, i ^ bit) for i in range(count)]


def pair_offsets(count):
    offsets = [0]
    bit = count // 2
    while bit:
        offsets += [offset ^ bit for offset in offsets]
        bit //= 2
    return offsets


def gather_pieces(own, axis):
    count = lax.axis_size(axis)
    pieces = [own]
    bit = count // 2
    while bit:
        pieces += [lax.ppermute(piece, axis, xor_pairs(count, bit)) for piece in pieces]
        bit //= 2
    return pieces


def across(count, step):
    moves = []
    for i in range(count):
        target = i + step if i % 2 == 0 else i - step
        if 0 <= target < count:
            moves.append((i, target))
    return moves


def tile_copies(tiles_hbm, tiles, sems, count):
    for b in range(count):
        pltpu.make_async_copy(tiles_hbm.at[b], tiles.at[b], sems.at[b]).start()


def block_at(index, side):
    return pl.ds(pl.multiple_of(index * side, side), side)


def forward_kernel(slot_ref, own, pair, diag, inv, tiles_hbm, agg, window, tiles, sems):
    blocks, slots, side, _ = tiles.shape
    nodes = own.shape[1]
    tile_copies(tiles_hbm, tiles, sems, blocks)
    window[:, :nodes] = own[...]
    window[:, nodes : 2 * nodes] = pair[...]
    window[:, 2 * nodes : 3 * nodes] = diag[...]
    window[:, 3 * nodes :] = jnp.zeros((own.shape[0], side), window.dtype)

    def block(b, carry):
        pltpu.make_async_copy(tiles_hbm.at[b], tiles.at[b], sems.at[b]).wait()
        total = None
        for t in range(0, slots, 2):
            taken = range(t, min(t + 2, slots))
            source = jnp.concatenate(
                [window[:, block_at(slot_ref[b, s], side)] for s in taken], axis=1
            )
            edges = jnp.concatenate([tiles[b, s] for s in taken], axis=1)
            part = lax.dot_general(source, edges, CONTRACT_LAST, preferred_element_type=jnp.float32)
            total = part if total is None else total + part
        here = block_at(b, side)
        agg[:, here] = (total * inv[:, here]).astype(agg.dtype)
        return carry

    lax.fori_loop(0, blocks, block, 0)


def backward_kernel(slot_ref, weight, inv, *refs, pieces):
    cots = refs[:pieces]
    tiles_hbm, own, pair, diag, acc, scaled, tiles, sems = refs[pieces:]
    blocks, slots, side, _ = tiles.shape
    nodes = own.shape[1]
    tile_copies(tiles_hbm, tiles, sems, blocks)
    acc[...] = jnp.zeros_like(acc)
    wide = 4 * side

    def mix(i, carry):
        here = pl.ds(pl.multiple_of(i * wide, wide), wide)
        cot = jnp.concatenate([c[:, here] for c in cots], axis=0)
        grad = jnp.dot(weight[...], cot, preferred_element_type=jnp.float32)
        scaled[:, here] = (grad * inv[:, here]).astype(scaled.dtype)
        return carry

    lax.fori_loop(0, nodes // wide, mix, 0)

    def block(b, carry):
        pltpu.make_async_copy(tiles_hbm.at[b], tiles.at[b], sems.at[b]).wait()
        grad = scaled[:, block_at(b, side)]
        places = [block_at(slot_ref[b, s], side) for s in range(slots)]
        sums = [acc[:, place] for place in places]
        for t in range(0, slots, 2):
            taken = range(t, min(t + 2, slots))
            edges = jnp.concatenate([tiles[b, s] for s in taken], axis=1)
            part = jnp.dot(grad, edges, preferred_element_type=jnp.float32)
            for k, s in enumerate(taken):
                acc[:, places[s]] = sums[s] + part[:, k * side : (k + 1) * side]
        return carry

    lax.fori_loop(0, blocks, block, 0)

    own[...] = acc[:, :nodes]
    pair[...] = acc[:, nodes : 2 * nodes].astype(pair.dtype)
    diag[...] = acc[:, 2 * nodes : 3 * nodes].astype(diag.dtype)


def shards(features, weight, cotangent, degree, tile_src, tile_count, tile_vals):
    width, nodes = features.shape
    blocks, slots, side, _ = tile_vals.shape
    rows = lax.axis_size("row")
    cols = lax.axis_size("col")
    row = lax.axis_index("row")
    col = lax.axis_index("col")
    offsets = pair_offsets(cols)
    vmem = pl.BlockSpec(memory_space=pltpu.VMEM)
    smem = pl.BlockSpec(memory_space=pltpu.SMEM)
    hbm = pl.BlockSpec(memory_space=pl.ANY)

    inv_root = lax.rsqrt(degree.astype(jnp.float32))[None, :]
    scaled = (features.astype(jnp.float32) * inv_root).astype(jnp.bfloat16)
    pair_scaled = lax.ppermute(scaled, "row", xor_pairs(rows, 1))
    diag_scaled = lax.ppermute(pair_scaled, "row", across(rows, 2))
    cots = gather_pieces(cotangent, "col")

    source_row = tile_src // blocks
    group = jnp.where(source_row == row, 0, jnp.where(source_row == (row ^ 1), 1, 2))
    live = jnp.arange(slots, dtype=jnp.int32)[None, :] < tile_count[:, None]
    slot_at = jnp.where(live, group * blocks + tile_src % blocks, 3 * blocks)

    def piece_of(offset):
        return (col ^ offset) * width

    mine = col * width
    weight_rows = lax.dynamic_slice_in_dim(weight, mine, width, 0)
    weight_cols = lax.dynamic_slice_in_dim(weight, mine, width, 1)
    weight_back = jnp.concatenate(
        [lax.dynamic_slice_in_dim(weight_rows, piece_of(o), width, 1) for o in offsets], axis=1
    )
    weight_out = jnp.concatenate(
        [lax.dynamic_slice_in_dim(weight_cols, piece_of(o), width, 0) for o in offsets], axis=0
    )

    params = pltpu.CompilerParams(vmem_limit_bytes=VMEM_BYTES)
    tile_scratch = [
        pltpu.VMEM(tile_vals.shape, tile_vals.dtype),
        pltpu.SemaphoreType.DMA((blocks,)),
    ]
    narrow = jax.ShapeDtypeStruct((width, nodes), jnp.bfloat16)
    full = jax.ShapeDtypeStruct((width, nodes), jnp.float32)
    own_grad, pair_grad, diag_grad = pl.pallas_call(
        functools.partial(backward_kernel, pieces=cols),
        out_shape=(full, narrow, narrow),
        in_specs=[smem, vmem, vmem] + [vmem] * cols + [hbm],
        out_specs=(vmem, vmem, vmem),
        scratch_shapes=[
            pltpu.VMEM((width, 3 * nodes + side), jnp.float32),
            pltpu.VMEM((width, nodes), jnp.bfloat16),
        ]
        + tile_scratch,
        compiler_params=params,
        name="backward_tiles",
    )(slot_at, weight_back, inv_root, *cots, tile_vals)
    relayed = lax.ppermute(diag_grad, "row", [(t, s) for s, t in across(rows, 2)])
    joined = (pair_grad.astype(jnp.float32) + relayed.astype(jnp.float32)).astype(jnp.bfloat16)
    returned = lax.ppermute(joined, "row", xor_pairs(rows, 1))

    aggregated = pl.pallas_call(
        forward_kernel,
        out_shape=narrow,
        in_specs=[smem, vmem, vmem, vmem, vmem, hbm],
        out_specs=vmem,
        scratch_shapes=[pltpu.VMEM((width, 3 * nodes + side), jnp.bfloat16)] + tile_scratch,
        compiler_params=params,
        name="forward_tiles",
    )(slot_at, scaled, pair_scaled, diag_scaled, inv_root, tile_vals)

    agg_pieces = gather_pieces(aggregated, "col")
    output = lax.dot_general(
        weight_out,
        jnp.concatenate(agg_pieces, axis=0),
        (((0,), (0,)), ((), ())),
        preferred_element_type=jnp.float32,
    ).astype(jnp.bfloat16)

    partial = [
        lax.dot_general(aggregated, c, CONTRACT_LAST, preferred_element_type=jnp.float32)
        for c in cots
    ]
    total = jnp.stack(partial)
    if rows & (rows - 1) == 0:
        bit = 1
        while bit < rows:
            total = total + lax.ppermute(total, "row", xor_pairs(rows, bit))
            bit *= 2
    else:
        total = lax.psum(total, "row")
    total = total / math.sqrt(nodes * rows)
    weight_grad = jnp.zeros((width * cols, width), jnp.float32)
    for k, offset in enumerate(offsets):
        block = total[k] if offset == 0 else lax.ppermute(total[k], "col", xor_pairs(cols, offset))
        weight_grad = lax.dynamic_update_slice_in_dim(weight_grad, block, piece_of(offset), 0)

    input_grad = (own_grad + returned.astype(jnp.float32)) * inv_root
    return (output, input_grad, weight_grad)


def solution(mesh):
    placed = (
        P("col", "row"),
        P(),
        P("col", "row"),
        P("row"),
        P("row", None),
        P("row"),
        P("row", None, None, None),
    )
    return jax.shard_map(
        shards,
        mesh=mesh,
        in_specs=placed,
        out_specs=(P("col", "row"), P("col", "row"), P(None, "col")),
        check_vma=False,
    )
```

```python
import functools
import math

import jax
import jax.numpy as jnp
from jax import lax
from jax.experimental import pallas as pl
from jax.experimental.pallas import tpu as pltpu
from jax.sharding import PartitionSpec as P

CONTRACT_LAST = (((1,), (1,)), ((), ()))
VMEM_BYTES = 40 * 1024 * 1024


def xor_pairs(count, bit):
    return [(i, i ^ bit) for i in range(count)]


def across(count, step):
    moves = []
    for i in range(count):
        target = i + step if i % 2 == 0 else i - step
        if 0 <= target < count:
            moves.append((i, target))
    return moves


def bits_of(count):
    bits = []
    bit = count // 2
    while bit:
        bits.append(bit)
        bit //= 2
    return bits


def pair_offsets(count):
    offsets = [0]
    for bit in bits_of(count):
        offsets += [offset ^ bit for offset in offsets]
    return offsets


def gather_pieces(own, axis, others=()):
    count = lax.axis_size(axis)
    pieces = [own]
    for bit in bits_of(count):
        sent = pieces[:1] + list(tied(pieces[1:], others)) if others else pieces
        pieces = pieces + [lax.ppermute(piece, axis, xor_pairs(count, bit)) for piece in sent]
    return pieces


def tied(values, others):
    return lax.optimization_barrier((tuple(values), tuple(others)))[0]


def far(value):
    return pltpu.with_memory_space_constraint(value, pltpu.HBM)


def block_at(index, side):
    return pl.ds(pl.multiple_of(index * side, side), side)


def slot_groups(slots):
    return [range(t, min(t + 2, slots)) for t in range(0, slots, 2)]


def start_tiles(tiles_hbm, tiles, sems):
    for b in range(tiles.shape[0]):
        pltpu.make_async_copy(tiles_hbm.at[b], tiles.at[b], sems.at[b]).start()


def each_block(block, tiles_hbm, tiles, sems, together):
    def step(i, carry):
        for k in range(together):
            b = i * together + k
            pltpu.make_async_copy(tiles_hbm.at[b], tiles.at[b], sems.at[b]).wait()
        for k in range(together):
            block(i * together + k)
        return carry

    lax.fori_loop(0, tiles.shape[0] // together, step, 0)


def backward_kernel(slot_ref, inv, weight_hbm, *refs, offsets, together):
    cots, refs = refs[: len(offsets)], refs[len(offsets) :]
    tiles_hbm, own_grad, pair_grad, diag_grad, acc, cot, scaled, weight, tiles, sems, in_sems = refs
    blocks, slots, side, _ = tiles.shape
    width, nodes = own_grad.shape
    col = lax.axis_index("col")
    arrivals = [pltpu.make_async_copy(weight_hbm.at[block_at(col, width)], weight, in_sems.at[0])]
    for k, (value, offset) in enumerate(zip(cots, offsets)):
        place = cot.at[block_at(col ^ offset, width)]
        arrivals.append(pltpu.make_async_copy(value, place, in_sems.at[k + 1]))
    for copy in arrivals:
        copy.start()
    start_tiles(tiles_hbm, tiles, sems)
    acc[...] = jnp.zeros_like(acc)
    for copy in arrivals:
        copy.wait()
    wide = 4 * side

    def mix(i, carry):
        here = pl.ds(pl.multiple_of(i * wide, wide), wide)
        grad = jnp.dot(weight[...], cot[:, here], preferred_element_type=jnp.float32)
        scaled[:, here] = (grad * inv[:, here]).astype(scaled.dtype)
        return carry

    lax.fori_loop(0, nodes // wide, mix, 0)

    def block(b):
        places = [block_at(slot_ref[b, s], side) for s in range(slots)]
        grad = scaled[:, block_at(b, side)]
        sums = [acc[:, place] for place in places]
        for group in slot_groups(slots):
            edges = jnp.concatenate([tiles[b, s] for s in group], axis=1)
            spread = jnp.dot(grad, edges, preferred_element_type=jnp.float32)
            for k, s in enumerate(group):
                acc[:, places[s]] = sums[s] + spread[:, k * side : (k + 1) * side]

    each_block(block, tiles_hbm, tiles, sems, together)
    diag_grad[...] = acc[:, 2 * nodes : 3 * nodes].astype(diag_grad.dtype)
    pair_grad[...] = acc[:, nodes : 2 * nodes].astype(pair_grad.dtype)
    own_grad[...] = acc[:, :nodes]


def forward_kernel(slot_ref, inv, own, pair, diag, tiles_hbm, agg, window, tiles, sems, in_sems, *, together):
    blocks, slots, side, _ = tiles.shape
    width, nodes = agg.shape
    arrivals = [
        pltpu.make_async_copy(value, window.at[:, k * nodes : (k + 1) * nodes], in_sems.at[k])
        for k, value in enumerate((own, pair, diag))
    ]
    for copy in arrivals:
        copy.start()
    start_tiles(tiles_hbm, tiles, sems)
    window[:, 3 * nodes :] = jnp.zeros((width, side), window.dtype)
    for copy in arrivals:
        copy.wait()

    def block(b):
        places = [block_at(slot_ref[b, s], side) for s in range(slots)]
        total = None
        for group in slot_groups(slots):
            source = jnp.concatenate([window[:, places[s]] for s in group], axis=1)
            edges = jnp.concatenate([tiles[b, s] for s in group], axis=1)
            part = lax.dot_general(source, edges, CONTRACT_LAST, preferred_element_type=jnp.float32)
            total = part if total is None else total + part
        here = block_at(b, side)
        agg[:, here] = (total * inv[:, here]).astype(agg.dtype)

    each_block(block, tiles_hbm, tiles, sems, together)


def outer_kernel(*refs):
    cots, agg, out = refs[:-2], refs[-2], refs[-1]
    out[...] = jnp.concatenate(
        [
            lax.dot_general(c[...], agg[...], CONTRACT_LAST, preferred_element_type=jnp.float32)
            for c in cots
        ],
        axis=1,
    )


def shards(features, weight, cotangent, degree, tile_src, tile_count, tile_vals):
    width, nodes = features.shape
    blocks, slots, side, _ = tile_vals.shape
    rows = lax.axis_size("row")
    cols = lax.axis_size("col")
    row = lax.axis_index("row")
    col = lax.axis_index("col")
    offsets = pair_offsets(cols)
    vmem = pl.BlockSpec(memory_space=pltpu.VMEM)
    smem = pl.BlockSpec(memory_space=pltpu.SMEM)
    hbm = pl.BlockSpec(memory_space=pl.ANY)
    params = pltpu.CompilerParams(vmem_limit_bytes=VMEM_BYTES)
    light = pl.CostEstimate(flops=1, bytes_accessed=1, transcendentals=0)
    narrow = jax.ShapeDtypeStruct((width, nodes), jnp.bfloat16)
    full = jax.ShapeDtypeStruct((width, nodes), jnp.float32)
    together = 2 if blocks % 2 == 0 else 1
    tile_scratch = [
        pltpu.VMEM(tile_vals.shape, tile_vals.dtype),
        pltpu.SemaphoreType.DMA((blocks,)),
    ]
    pairs = xor_pairs(rows, 1)
    outward = across(rows, 2)
    inward = [(target, source) for source, target in outward]

    inv_root = lax.rsqrt(degree.astype(jnp.float32))[None, :]
    scaled = (features.astype(jnp.float32) * inv_root).astype(jnp.bfloat16)
    pair_scaled = lax.ppermute(scaled, "row", pairs)
    diag_scaled = lax.ppermute(pair_scaled, "row", outward)
    cots = gather_pieces(cotangent, "col")

    source_row = tile_src // blocks
    group = jnp.where(source_row == row, 0, jnp.where(source_row == (row ^ 1), 1, 2))
    live = jnp.arange(slots, dtype=jnp.int32)[None, :] < tile_count[:, None]
    slot_at = jnp.where(live, group * blocks + tile_src % blocks, 3 * blocks)
    weight_cols = lax.dynamic_slice_in_dim(weight, col * width, width, 1)

    cots_here = tied(cots[1:], (pair_scaled,))
    own_grad, pair_grad, diag_grad = pl.pallas_call(
        functools.partial(backward_kernel, offsets=offsets, together=together),
        out_shape=(full, narrow, narrow),
        in_specs=[smem, vmem] + [hbm] * (cols + 2),
        out_specs=(vmem,) * 3,
        scratch_shapes=[
            pltpu.VMEM((width, 3 * nodes + side), jnp.float32),
            pltpu.VMEM((width * cols, nodes), jnp.bfloat16),
            pltpu.VMEM((width, nodes), jnp.bfloat16),
            pltpu.VMEM((width, width * cols), jnp.bfloat16),
        ]
        + tile_scratch
        + [pltpu.SemaphoreType.DMA((cols + 1,))],
        compiler_params=params,
        cost_estimate=light,
        name="backward_tiles",
    )(slot_at, inv_root, far(weight), far(cotangent), *cots_here, far(tile_vals))

    halos = tied((scaled, pair_scaled, diag_scaled), (diag_grad,))
    aggregated = pl.pallas_call(
        functools.partial(forward_kernel, together=together),
        out_shape=narrow,
        in_specs=[smem, vmem] + [hbm] * 4,
        out_specs=vmem,
        scratch_shapes=[pltpu.VMEM((width, 3 * nodes + side), jnp.bfloat16)]
        + tile_scratch
        + [pltpu.SemaphoreType.DMA((3,))],
        compiler_params=params,
        cost_estimate=light,
        name="forward_tiles",
    )(slot_at, inv_root, *halos, far(tile_vals))

    relayed = lax.ppermute(diag_grad, "row", inward)
    (relayed,) = tied((relayed,), (aggregated,))
    joined = (pair_grad.astype(jnp.float32) + relayed.astype(jnp.float32)).astype(jnp.bfloat16)
    returned = lax.ppermute(joined, "row", pairs)
    input_grad = (own_grad + returned.astype(jnp.float32)) * inv_root

    agg_pieces = gather_pieces(aggregated, "col")
    weight_parts = jnp.stack(
        [lax.dynamic_slice_in_dim(weight_cols, (col ^ o) * width, width, 0) for o in offsets]
    )
    output = lax.dot_general(
        weight_parts.reshape(cols * width, width),
        jnp.concatenate(agg_pieces, axis=0),
        (((0,), (0,)), ((), ())),
        preferred_element_type=jnp.float32,
    ).astype(jnp.bfloat16)

    (late,) = tied((aggregated,), (joined,))
    outer = pl.pallas_call(
        outer_kernel,
        out_shape=jax.ShapeDtypeStruct((width, cols * width), jnp.float32),
        in_specs=[vmem] * (cols + 1),
        out_specs=vmem,
        compiler_params=pltpu.CompilerParams(vmem_limit_bytes=VMEM_BYTES // 4),
        cost_estimate=light,
        name="outer_product",
    )(*cots, late)
    row_bits = bits_of(rows) if rows & (rows - 1) == 0 else []
    if not row_bits:
        outer = lax.psum(outer, "row")
    for bit in row_bits[-2::-1]:
        outer = outer + lax.ppermute(outer, "row", xor_pairs(rows, bit))
    known = [0]
    blocks_of = {o: outer[:, k * width : (k + 1) * width] for k, o in enumerate(offsets)}
    for bit in reversed(bits_of(cols)):
        kept = [o for o in blocks_of if not o & bit]
        sent = jnp.stack([blocks_of[o | bit] for o in kept])
        (sent,) = tied((sent,), (agg_pieces[1], returned))
        other = lax.ppermute(sent, "col", xor_pairs(cols, bit))
        blocks_of = {o: jnp.concatenate([blocks_of[o], other[k]], axis=1) for k, o in enumerate(kept)}
        known = known + [o ^ bit for o in known]
    total = blocks_of[0]
    if row_bits:
        total = total + lax.ppermute(total, "row", pairs)
    place = jnp.asarray([known.index(o) for o in range(cols)], jnp.int32)
    weight_grad = jnp.concatenate(
        [
            lax.dynamic_slice_in_dim(total, place[col ^ c] * width, width, 1)
            for c in range(cols)
        ],
        axis=1,
    ) / math.sqrt(nodes * rows)
    return (output, input_grad, weight_grad.T)


def solution(mesh):
    placed = (
        P("col", "row"),
        P(),
        P("col", "row"),
        P("row"),
        P("row", None),
        P("row"),
        P("row", None, None, None),
    )
    return jax.shard_map(
        shards,
        mesh=mesh,
        in_specs=placed,
        out_specs=(P("col", "row"), P("col", "row"), P(None, "col")),
        check_vma=False,
    )
```

```python
import functools
import math

import jax
import jax.numpy as jnp
from jax import lax
from jax.experimental import pallas as pl
from jax.experimental.pallas import tpu as pltpu
from jax.sharding import PartitionSpec as P

CONTRACT_LAST = (((1,), (1,)), ((), ()))
VMEM_BYTES = 40 * 1024 * 1024


def xor_pairs(count, bit):
    return [(i, i ^ bit) for i in range(count)]


def across(count, step):
    moves = []
    for i in range(count):
        target = i + step if i % 2 == 0 else i - step
        if 0 <= target < count:
            moves.append((i, target))
    return moves


def bits_of(count):
    bits = []
    bit = count // 2
    while bit:
        bits.append(bit)
        bit //= 2
    return bits


def pair_offsets(count):
    offsets = [0]
    for bit in bits_of(count):
        offsets += [offset ^ bit for offset in offsets]
    return offsets


def gather_pieces(own, axis, others=()):
    count = lax.axis_size(axis)
    pieces = [own]
    for bit in bits_of(count):
        sent = pieces[:1] + list(tied(pieces[1:], others)) if others else pieces
        pieces = pieces + [lax.ppermute(piece, axis, xor_pairs(count, bit)) for piece in sent]
    return pieces


def tied(values, others):
    return lax.optimization_barrier((tuple(values), tuple(others)))[0]


def far(value):
    return pltpu.with_memory_space_constraint(value, pltpu.HBM)


def block_at(index, side):
    return pl.ds(pl.multiple_of(index * side, side), side)


def slot_groups(slots):
    return [range(t, min(t + 2, slots)) for t in range(0, slots, 2)]


def start_tiles(tiles_hbm, tiles, sems, first, last):
    for b in range(first, last):
        pltpu.make_async_copy(tiles_hbm.at[b], tiles.at[b], sems.at[b]).start()


def each_block(block, tiles_hbm, tiles, sems, together):
    def step(i, carry):
        for k in range(together):
            b = i * together + k
            pltpu.make_async_copy(tiles_hbm.at[b], tiles.at[b], sems.at[b]).wait()
        for k in range(together):
            block(i * together + k)
        return carry

    lax.fori_loop(0, tiles.shape[0] // together, step, 0)


def backward_kernel(slot_ref, inv, weight_hbm, *refs, offsets, together):
    cots, refs = refs[: len(offsets)], refs[len(offsets) :]
    tiles_hbm, own_grad, pair_grad, diag_grad, acc, cot, scaled, weight, tiles, sems, in_sems = refs
    blocks, slots, side, _ = tiles.shape
    width, nodes = own_grad.shape
    col = lax.axis_index("col")
    arrivals = [pltpu.make_async_copy(weight_hbm.at[block_at(col, width)], weight, in_sems.at[0])]
    for k, (value, offset) in enumerate(zip(cots, offsets)):
        place = cot.at[block_at(col ^ offset, width)]
        arrivals.append(pltpu.make_async_copy(value, place, in_sems.at[k + 1]))
    for copy in arrivals:
        copy.start()
    start_tiles(tiles_hbm, tiles, sems, 0, blocks)
    acc[...] = jnp.zeros_like(acc)
    for copy in arrivals:
        copy.wait()
    wide = 4 * side

    def mix(i, carry):
        here = pl.ds(pl.multiple_of(i * wide, wide), wide)
        grad = jnp.dot(weight[...], cot[:, here], preferred_element_type=jnp.float32)
        scaled[:, here] = (grad * inv[:, here]).astype(scaled.dtype)
        return carry

    lax.fori_loop(0, nodes // wide, mix, 0)

    def block(b):
        places = [block_at(slot_ref[b, s], side) for s in range(slots)]
        grad = scaled[:, block_at(b, side)]
        sums = [acc[:, place] for place in places]
        for group in slot_groups(slots):
            edges = jnp.concatenate([tiles[b, s] for s in group], axis=1)
            spread = jnp.dot(grad, edges, preferred_element_type=jnp.float32)
            for k, s in enumerate(group):
                acc[:, places[s]] = sums[s] + spread[:, k * side : (k + 1) * side]

    each_block(block, tiles_hbm, tiles, sems, together)
    diag_grad[...] = acc[:, 2 * nodes : 3 * nodes].astype(diag_grad.dtype)
    pair_grad[...] = acc[:, nodes : 2 * nodes].astype(pair_grad.dtype)
    own_grad[...] = acc[:, :nodes]


def forward_kernel(slot_ref, inv, own, pair, diag, tiles_hbm, agg, window, tiles, sems, in_sems, *, together):
    blocks, slots, side, _ = tiles.shape
    width, nodes = agg.shape
    arrivals = [
        pltpu.make_async_copy(value, window.at[:, k * nodes : (k + 1) * nodes], in_sems.at[k])
        for k, value in enumerate((own, pair, diag))
    ]
    for copy in arrivals:
        copy.start()
    start_tiles(tiles_hbm, tiles, sems, 0, together)
    window[:, 3 * nodes :] = jnp.zeros((width, side), window.dtype)
    for copy in arrivals:
        copy.wait()
    start_tiles(tiles_hbm, tiles, sems, together, blocks)

    def block(b):
        places = [block_at(slot_ref[b, s], side) for s in range(slots)]
        total = None
        for group in slot_groups(slots):
            source = jnp.concatenate([window[:, places[s]] for s in group], axis=1)
            edges = jnp.concatenate([tiles[b, s] for s in group], axis=1)
            part = lax.dot_general(source, edges, CONTRACT_LAST, preferred_element_type=jnp.float32)
            total = part if total is None else total + part
        here = block_at(b, side)
        agg[:, here] = (total * inv[:, here]).astype(agg.dtype)

    each_block(block, tiles_hbm, tiles, sems, together)


def outer_kernel(*refs):
    cots, agg, out = refs[:-2], refs[-2], refs[-1]
    out[...] = jnp.concatenate(
        [
            lax.dot_general(c[...], agg[...], CONTRACT_LAST, preferred_element_type=jnp.float32)
            for c in cots
        ],
        axis=1,
    )


def shards(features, weight, cotangent, degree, tile_src, tile_count, tile_vals):
    width, nodes = features.shape
    blocks, slots, side, _ = tile_vals.shape
    rows = lax.axis_size("row")
    cols = lax.axis_size("col")
    row = lax.axis_index("row")
    col = lax.axis_index("col")
    offsets = pair_offsets(cols)
    vmem = pl.BlockSpec(memory_space=pltpu.VMEM)
    smem = pl.BlockSpec(memory_space=pltpu.SMEM)
    hbm = pl.BlockSpec(memory_space=pl.ANY)
    params = pltpu.CompilerParams(vmem_limit_bytes=VMEM_BYTES)
    light = pl.CostEstimate(flops=1, bytes_accessed=1, transcendentals=0)
    narrow = jax.ShapeDtypeStruct((width, nodes), jnp.bfloat16)
    full = jax.ShapeDtypeStruct((width, nodes), jnp.float32)
    together = math.gcd(blocks, 8)
    tile_scratch = [
        pltpu.VMEM(tile_vals.shape, tile_vals.dtype),
        pltpu.SemaphoreType.DMA((blocks,)),
    ]
    pairs = xor_pairs(rows, 1)
    outward = across(rows, 2)
    inward = [(target, source) for source, target in outward]

    inv_root = lax.rsqrt(degree.astype(jnp.float32))[None, :]
    scaled = (features.astype(jnp.float32) * inv_root).astype(jnp.bfloat16)
    pair_scaled = lax.ppermute(scaled, "row", pairs)
    diag_scaled = lax.ppermute(pair_scaled, "row", outward)
    source_row = tile_src // blocks
    group = jnp.where(source_row == row, 0, jnp.where(source_row == (row ^ 1), 1, 2))
    live = jnp.arange(slots, dtype=jnp.int32)[None, :] < tile_count[:, None]
    slot_at = jnp.where(live, group * blocks + tile_src % blocks, 3 * blocks)
    cots = gather_pieces(cotangent, "col", (slot_at,))
    weight_cols = lax.dynamic_slice_in_dim(weight, col * width, width, 1)

    cots_here = tied(cots[1:], (pair_scaled,))
    own_grad, pair_grad, diag_grad = pl.pallas_call(
        functools.partial(backward_kernel, offsets=offsets, together=together),
        out_shape=(full, narrow, narrow),
        in_specs=[smem, vmem] + [hbm] * (cols + 2),
        out_specs=(vmem,) * 3,
        scratch_shapes=[
            pltpu.VMEM((width, 3 * nodes + side), jnp.float32),
            pltpu.VMEM((width * cols, nodes), jnp.bfloat16),
            pltpu.VMEM((width, nodes), jnp.bfloat16),
            pltpu.VMEM((width, width * cols), jnp.bfloat16),
        ]
        + tile_scratch
        + [pltpu.SemaphoreType.DMA((cols + 1,))],
        compiler_params=params,
        cost_estimate=light,
        name="backward_tiles",
    )(slot_at, inv_root, far(weight), far(cotangent), *cots_here, far(tile_vals))

    halos = tied((scaled, pair_scaled, diag_scaled), (diag_grad,))
    aggregated = pl.pallas_call(
        functools.partial(forward_kernel, together=together),
        out_shape=narrow,
        in_specs=[smem, vmem] + [hbm] * 4,
        out_specs=vmem,
        scratch_shapes=[pltpu.VMEM((width, 3 * nodes + side), jnp.bfloat16)]
        + tile_scratch
        + [pltpu.SemaphoreType.DMA((3,))],
        compiler_params=params,
        cost_estimate=light,
        name="forward_tiles",
    )(slot_at, inv_root, *halos, far(tile_vals))

    relayed = lax.ppermute(diag_grad, "row", inward)
    (relayed,) = tied((relayed,), (aggregated,))
    joined = (pair_grad.astype(jnp.float32) + relayed.astype(jnp.float32)).astype(jnp.bfloat16)
    returned = lax.ppermute(joined, "row", pairs)
    input_grad = (own_grad + returned.astype(jnp.float32)) * inv_root

    agg_pieces = gather_pieces(aggregated, "col")
    weight_parts = jnp.stack(
        [lax.dynamic_slice_in_dim(weight_cols, (col ^ o) * width, width, 0) for o in offsets]
    )
    output = lax.dot_general(
        weight_parts.reshape(cols * width, width),
        jnp.concatenate(agg_pieces, axis=0),
        (((0,), (0,)), ((), ())),
        preferred_element_type=jnp.float32,
    ).astype(jnp.bfloat16)

    outer = pl.pallas_call(
        outer_kernel,
        out_shape=jax.ShapeDtypeStruct((width, cols * width), jnp.float32),
        in_specs=[vmem] * (cols + 1),
        out_specs=vmem,
        compiler_params=pltpu.CompilerParams(vmem_limit_bytes=VMEM_BYTES // 4),
        cost_estimate=light,
        name="outer_product",
    )(*cots, aggregated)
    row_bits = bits_of(rows) if rows & (rows - 1) == 0 else []
    if not row_bits:
        outer = lax.psum(outer, "row")

    def over_rows(value, bits, after):
        for bit, others in zip(bits, after):
            if others:
                (value,) = tied((value,), others)
            value = value + lax.ppermute(value, "row", xor_pairs(rows, bit))
        return value

    def over_chips(value, bits, others):
        if others:
            (value,) = tied((value,), others)
        steps = [0]
        for bit in bits:
            steps += [step | bit for step in steps]
        return value + sum(
            lax.ppermute(value, "row", xor_pairs(rows, step)) for step in steps[1:]
        ) if steps[1:] else value

    known = [0]
    outer = over_rows(outer, row_bits[-1:], [()] * len(row_bits))
    blocks_of = {o: outer[:, k * width : (k + 1) * width] for k, o in enumerate(offsets)}
    for bit in reversed(bits_of(cols)):
        kept = [o for o in blocks_of if not o & bit]
        both = jnp.stack([blocks_of[o] for o in kept] + [blocks_of[o | bit] for o in kept])
        if 2 * bit == cols:
            both = over_rows(both, row_bits[-2::-1], [(joined,)] + [()] * len(row_bits))
            (both,) = tied((both,), (agg_pieces[1], returned))
        other = lax.ppermute(both[len(kept) :], "col", xor_pairs(cols, bit))
        blocks_of = {
            o: jnp.concatenate([both[k], other[k]], axis=1) for k, o in enumerate(kept)
        }
        known = known + [o ^ bit for o in known]
    total = blocks_of[0]
    pass
    place = jnp.asarray([known.index(o) for o in range(cols)], jnp.int32)
    weight_grad = jnp.concatenate(
        [
            lax.dynamic_slice_in_dim(total, place[col ^ c] * width, width, 1)
            for c in range(cols)
        ],
        axis=1,
    ) / math.sqrt(nodes * rows)
    return (output, input_grad, weight_grad.T)


def solution(mesh):
    placed = (
        P("col", "row"),
        P(),
        P("col", "row"),
        P("row"),
        P("row", None),
        P("row"),
        P("row", None, None, None),
    )
    return jax.shard_map(
        shards,
        mesh=mesh,
        in_specs=placed,
        out_specs=(P("col", "row"), P("col", "row"), P(None, "col")),
        check_vma=False,
    )
```

```python
import functools
import math

import jax
import jax.numpy as jnp
from jax import lax
from jax.experimental import pallas as pl
from jax.experimental.pallas import tpu as pltpu
from jax.sharding import PartitionSpec as P

CONTRACT_LAST = (((1,), (1,)), ((), ()))
VMEM_BYTES = 40 * 1024 * 1024


def xor_pairs(count, bit):
    return [(i, i ^ bit) for i in range(count)]


def across(count, step):
    moves = []
    for i in range(count):
        target = i + step if i % 2 == 0 else i - step
        if 0 <= target < count:
            moves.append((i, target))
    return moves


def bits_of(count):
    bits = []
    bit = count // 2
    while bit:
        bits.append(bit)
        bit //= 2
    return bits


def pair_offsets(count):
    offsets = [0]
    for bit in bits_of(count):
        offsets += [offset ^ bit for offset in offsets]
    return offsets


def gather_pieces(own, axis, others=()):
    count = lax.axis_size(axis)
    pieces = [own]
    for bit in bits_of(count):
        sent = pieces[:1] + list(tied(pieces[1:], others)) if others else pieces
        pieces = pieces + [lax.ppermute(piece, axis, xor_pairs(count, bit)) for piece in sent]
    return pieces


def tied(values, others):
    return lax.optimization_barrier((tuple(values), tuple(others)))[0]


def far(value):
    return pltpu.with_memory_space_constraint(value, pltpu.HBM)


def block_at(index, side):
    return pl.ds(pl.multiple_of(index * side, side), side)


def slot_groups(slots):
    return [range(t, min(t + 2, slots)) for t in range(0, slots, 2)]


def start_tiles(tiles_hbm, tiles, sems, first, last):
    for b in range(first, last):
        pltpu.make_async_copy(tiles_hbm.at[b], tiles.at[b], sems.at[b]).start()


def each_block(block, tiles_hbm, tiles, sems, together, before=None):
    side = tiles.shape[2]

    def step(i, carry):
        given = before(i * together) if before else None
        for k in range(together):
            b = i * together + k
            pltpu.make_async_copy(tiles_hbm.at[b], tiles.at[b], sems.at[b]).wait()
        for k in range(together):
            if before:
                block(i * together + k, given[:, k * side : (k + 1) * side])
            else:
                block(i * together + k)
        return carry

    lax.fori_loop(0, tiles.shape[0] // together, step, 0)


def scale_kernel(degree_hbm, features_hbm, scaled, inv, degree, features, sems):
    width = scaled.shape[0]
    halves = [slice(0, width // 2), slice(width // 2, width)]
    copies = [pltpu.make_async_copy(degree_hbm, degree, sems.at[0])]
    for k, half in enumerate(halves):
        copies.append(pltpu.make_async_copy(features_hbm.at[half], features.at[half], sems.at[k + 1]))
    for copy in copies:
        copy.start()
    copies[0].wait()
    inv[...] = lax.rsqrt(degree[...].astype(jnp.float32))
    for copy, half in zip(copies[1:], halves):
        copy.wait()
        scaled[half, :] = (features[half, :].astype(jnp.float32) * inv[...]).astype(scaled.dtype)


def backward_kernel(slot_ref, inv, weight_hbm, *refs, offsets, together):
    cots, refs = refs[: len(offsets)], refs[len(offsets) :]
    tiles_hbm, own_grad, pair_grad, diag_grad, acc, cot, weight, near, tiles, sems, in_sems, out_sems = refs
    blocks, slots, side, _ = tiles.shape
    width, nodes = own_grad.shape
    col = lax.axis_index("col")
    arrivals = [pltpu.make_async_copy(weight_hbm.at[block_at(col, width)], weight, in_sems.at[0])]
    for k, (value, offset) in enumerate(zip(cots, offsets)):
        place = cot.at[block_at(col ^ offset, width)]
        arrivals.append(pltpu.make_async_copy(value, place, in_sems.at[k + 1]))
    for copy in arrivals:
        copy.start()
    start_tiles(tiles_hbm, tiles, sems, 0, blocks)
    acc[...] = jnp.zeros_like(acc)
    for copy in arrivals:
        copy.wait()
    def mixed(first):
        here = pl.ds(pl.multiple_of(first * side, together * side), together * side)
        grad = jnp.dot(weight[...], cot[:, here], preferred_element_type=jnp.float32)
        return (grad * inv[:, here]).astype(cot.dtype)

    def block(b, grad):
        places = [block_at(slot_ref[b, s], side) for s in range(slots)]
        sums = [acc[:, place] for place in places]
        for group in slot_groups(slots):
            edges = jnp.concatenate([tiles[b, s] for s in group], axis=1)
            spread = jnp.dot(grad, edges, preferred_element_type=jnp.float32)
            for k, s in enumerate(group):
                acc[:, places[s]] = sums[s] + spread[:, k * side : (k + 1) * side]

    each_block(block, tiles_hbm, tiles, sems, together, mixed)
    own_copy = pltpu.make_async_copy(acc.at[:, :nodes], own_grad, out_sems.at[0])
    own_copy.start()
    near[...] = acc[:, nodes : 2 * nodes].astype(near.dtype)
    near_copy = pltpu.make_async_copy(near, pair_grad, out_sems.at[1])
    near_copy.start()
    diag_grad[...] = acc[:, 2 * nodes : 3 * nodes].astype(diag_grad.dtype)
    own_copy.wait()
    near_copy.wait()


def forward_kernel(slot_ref, inv, own, pair, diag, tiles_hbm, agg, window, tiles, sems, in_sems, *, together):
    blocks, slots, side, _ = tiles.shape
    width, nodes = agg.shape
    arrivals = [
        pltpu.make_async_copy(value, window.at[:, k * nodes : (k + 1) * nodes], in_sems.at[k])
        for k, value in enumerate((own, pair, diag))
    ]
    for copy in arrivals:
        copy.start()
    start_tiles(tiles_hbm, tiles, sems, 0, together)
    window[:, 3 * nodes :] = jnp.zeros((width, side), window.dtype)
    for copy in arrivals:
        copy.wait()
    start_tiles(tiles_hbm, tiles, sems, together, blocks)

    def block(b):
        places = [block_at(slot_ref[b, s], side) for s in range(slots)]
        total = None
        for group in slot_groups(slots):
            source = jnp.concatenate([window[:, places[s]] for s in group], axis=1)
            edges = jnp.concatenate([tiles[b, s] for s in group], axis=1)
            part = lax.dot_general(source, edges, CONTRACT_LAST, preferred_element_type=jnp.float32)
            total = part if total is None else total + part
        here = block_at(b, side)
        agg[:, here] = (total * inv[:, here]).astype(agg.dtype)

    each_block(block, tiles_hbm, tiles, sems, together)


def outer_kernel(*refs):
    cots, agg, out = refs[:-2], refs[-2], refs[-1]
    out[...] = jnp.concatenate(
        [
            lax.dot_general(c[...], agg[...], CONTRACT_LAST, preferred_element_type=jnp.float32)
            for c in cots
        ],
        axis=1,
    )


def shards(features, weight, cotangent, degree, tile_src, tile_count, tile_vals):
    width, nodes = features.shape
    blocks, slots, side, _ = tile_vals.shape
    rows = lax.axis_size("row")
    cols = lax.axis_size("col")
    row = lax.axis_index("row")
    col = lax.axis_index("col")
    offsets = pair_offsets(cols)
    vmem = pl.BlockSpec(memory_space=pltpu.VMEM)
    smem = pl.BlockSpec(memory_space=pltpu.SMEM)
    hbm = pl.BlockSpec(memory_space=pl.ANY)
    params = pltpu.CompilerParams(vmem_limit_bytes=VMEM_BYTES)
    light = pl.CostEstimate(flops=1, bytes_accessed=1, transcendentals=0)
    narrow = jax.ShapeDtypeStruct((width, nodes), jnp.bfloat16)
    full = jax.ShapeDtypeStruct((width, nodes), jnp.float32)
    together = math.gcd(blocks, 8)
    tile_scratch = [
        pltpu.VMEM(tile_vals.shape, tile_vals.dtype),
        pltpu.SemaphoreType.DMA((blocks,)),
    ]
    pairs = xor_pairs(rows, 1)
    outward = across(rows, 2)
    inward = [(target, source) for source, target in outward]

    scaled, inv_root = pl.pallas_call(
        scale_kernel,
        out_shape=(narrow, jax.ShapeDtypeStruct((1, nodes), jnp.float32)),
        in_specs=[hbm, hbm],
        out_specs=(vmem, vmem),
        scratch_shapes=[
            pltpu.VMEM((1, nodes), degree.dtype),
            pltpu.VMEM((width, nodes), features.dtype),
            pltpu.SemaphoreType.DMA((3,)),
        ],
        compiler_params=pltpu.CompilerParams(vmem_limit_bytes=VMEM_BYTES // 8),
        cost_estimate=light,
        name="scale",
    )(far(degree[None, :]), far(features))
    pair_scaled = lax.ppermute(scaled, "row", pairs)
    diag_scaled = lax.ppermute(pair_scaled, "row", outward)
    source_row = tile_src // blocks
    group = jnp.where(source_row == row, 0, jnp.where(source_row == (row ^ 1), 1, 2))
    live = jnp.arange(slots, dtype=jnp.int32)[None, :] < tile_count[:, None]
    slot_at = jnp.where(live, group * blocks + tile_src % blocks, 3 * blocks)
    cots = gather_pieces(cotangent, "col", (slot_at,))
    weight_cols = lax.dynamic_slice_in_dim(weight, col * width, width, 1)

    cots_here = tied(cots[1:], (pair_scaled,))
    own_grad, pair_grad, diag_grad = pl.pallas_call(
        functools.partial(backward_kernel, offsets=offsets, together=together),
        out_shape=(
            pltpu.HBM(full.shape, full.dtype),
            pltpu.HBM(narrow.shape, narrow.dtype),
            narrow,
        ),
        in_specs=[smem, vmem] + [hbm] * (cols + 2),
        out_specs=(hbm, hbm, vmem),
        scratch_shapes=[
            pltpu.VMEM((width, 3 * nodes + side), jnp.float32),
            pltpu.VMEM((width * cols, nodes), jnp.bfloat16),
            pltpu.VMEM((width, width * cols), jnp.bfloat16),
            pltpu.VMEM((width, nodes), jnp.bfloat16),
        ]
        + tile_scratch
        + [pltpu.SemaphoreType.DMA((cols + 1,)), pltpu.SemaphoreType.DMA((2,))],
        compiler_params=params,
        cost_estimate=light,
        name="backward_tiles",
    )(slot_at, inv_root, far(weight), far(cotangent), *cots_here, far(tile_vals))

    halos = tied((scaled, pair_scaled, diag_scaled), (diag_grad,))
    aggregated = pl.pallas_call(
        functools.partial(forward_kernel, together=together),
        out_shape=narrow,
        in_specs=[smem, vmem] + [hbm] * 4,
        out_specs=vmem,
        scratch_shapes=[pltpu.VMEM((width, 3 * nodes + side), jnp.bfloat16)]
        + tile_scratch
        + [pltpu.SemaphoreType.DMA((3,))],
        compiler_params=params,
        cost_estimate=light,
        name="forward_tiles",
    )(slot_at, inv_root, *halos, far(tile_vals))

    relayed = lax.ppermute(diag_grad, "row", inward)
    (relayed,) = tied((relayed,), (aggregated,))
    joined = (pair_grad.astype(jnp.float32) + relayed.astype(jnp.float32)).astype(jnp.bfloat16)
    returned = lax.ppermute(joined, "row", pairs)
    input_grad = (own_grad + returned.astype(jnp.float32)) * inv_root

    agg_pieces = gather_pieces(aggregated, "col")
    weight_parts = jnp.stack(
        [lax.dynamic_slice_in_dim(weight_cols, (col ^ o) * width, width, 0) for o in offsets]
    )
    output = lax.dot_general(
        weight_parts.reshape(cols * width, width),
        jnp.concatenate(agg_pieces, axis=0),
        (((0,), (0,)), ((), ())),
        preferred_element_type=jnp.float32,
    ).astype(jnp.bfloat16)

    outer = pl.pallas_call(
        outer_kernel,
        out_shape=jax.ShapeDtypeStruct((width, cols * width), jnp.float32),
        in_specs=[vmem] * (cols + 1),
        out_specs=vmem,
        compiler_params=pltpu.CompilerParams(vmem_limit_bytes=VMEM_BYTES // 4),
        cost_estimate=light,
        name="outer_product",
    )(*cots, aggregated)
    row_bits = bits_of(rows) if rows & (rows - 1) == 0 else []
    if not row_bits:
        outer = lax.psum(outer, "row")

    def over_rows(value, bits, after):
        for bit, others in zip(bits, after):
            if others:
                (value,) = tied((value,), others)
            value = value + lax.ppermute(value, "row", xor_pairs(rows, bit))
        return value

    known = [0]
    outer = over_rows(outer, row_bits[-1:], [()] * len(row_bits))
    blocks_of = {o: outer[:, k * width : (k + 1) * width] for k, o in enumerate(offsets)}
    for bit in reversed(bits_of(cols)):
        kept = [o for o in blocks_of if not o & bit]
        both = jnp.stack([blocks_of[o] for o in kept] + [blocks_of[o | bit] for o in kept])
        if 2 * bit == cols:
            both = over_rows(both, row_bits[-2::-1], [(joined,)] + [()] * len(row_bits))
            (both,) = tied((both,), (agg_pieces[1], returned))
        other = lax.ppermute(both[len(kept) :], "col", xor_pairs(cols, bit))
        blocks_of = {
            o: jnp.concatenate([both[k], other[k]], axis=1) for k, o in enumerate(kept)
        }
        known = known + [o ^ bit for o in known]
    total = blocks_of[0]
    place = jnp.asarray([known.index(o) for o in range(cols)], jnp.int32)
    weight_grad = jnp.concatenate(
        [
            lax.dynamic_slice_in_dim(total, place[col ^ c] * width, width, 1)
            for c in range(cols)
        ],
        axis=1,
    ) / math.sqrt(nodes * rows)
    return (output, input_grad, weight_grad.T)


def solution(mesh):
    placed = (
        P("col", "row"),
        P(),
        P("col", "row"),
        P("row"),
        P("row", None),
        P("row"),
        P("row", None, None, None),
    )
    return jax.shard_map(
        shards,
        mesh=mesh,
        in_specs=placed,
        out_specs=(P("col", "row"), P("col", "row"), P(None, "col")),
        check_vma=False,
    )
```

```python
import functools
import math

import jax
import jax.numpy as jnp
from jax import lax
from jax.experimental import pallas as pl
from jax.experimental.pallas import tpu as pltpu
from jax.sharding import PartitionSpec as P

CONTRACT_LAST = (((1,), (1,)), ((), ()))
VMEM_BYTES = 32 * 1024 * 1024


def xor_pairs(count, bit):
    return [(i, i ^ bit) for i in range(count)]


def across(count, step):
    moves = []
    for i in range(count):
        target = i + step if i % 2 == 0 else i - step
        if 0 <= target < count:
            moves.append((i, target))
    return moves


def bits_of(count):
    bits = []
    bit = count // 2
    while bit:
        bits.append(bit)
        bit //= 2
    return bits


def pair_offsets(count):
    offsets = [0]
    for bit in bits_of(count):
        offsets += [offset ^ bit for offset in offsets]
    return offsets


def gather_pieces(own, axis, others=()):
    count = lax.axis_size(axis)
    pieces = [own]
    for bit in bits_of(count):
        sent = pieces[:1] + list(tied(pieces[1:], others)) if others else pieces
        pieces = pieces + [lax.ppermute(piece, axis, xor_pairs(count, bit)) for piece in sent]
    return pieces


def tied(values, others):
    return lax.optimization_barrier((tuple(values), tuple(others)))[0]


def far(value):
    return pltpu.with_memory_space_constraint(value, pltpu.HBM)


def block_at(index, side):
    return pl.ds(pl.multiple_of(index * side, side), side)


def slot_groups(slots):
    return [range(t, min(t + 2, slots)) for t in range(0, slots, 2)]


def start_tiles(tiles_hbm, tiles, sems, first, last):
    for b in range(first, last):
        pltpu.make_async_copy(tiles_hbm.at[b], tiles.at[b], sems.at[b]).start()


def each_block(block, tiles_hbm, tiles, sems, together, before=None):
    side = tiles.shape[2]

    def step(i, carry):
        given = before(i * together) if before else None
        for k in range(together):
            b = i * together + k
            pltpu.make_async_copy(tiles_hbm.at[b], tiles.at[b], sems.at[b]).wait()
        for k in range(together):
            if before:
                block(i * together + k, given[:, k * side : (k + 1) * side])
            else:
                block(i * together + k)
        return carry

    lax.fori_loop(0, tiles.shape[0] // together, step, 0)


def scale_kernel(degree_hbm, features_hbm, scaled, inv, degree, features, sems):
    width = scaled.shape[0]
    halves = [slice(0, width // 2), slice(width // 2, width)]
    copies = [pltpu.make_async_copy(degree_hbm, degree, sems.at[0])]
    for k, half in enumerate(halves):
        copies.append(pltpu.make_async_copy(features_hbm.at[half], features.at[half], sems.at[k + 1]))
    for copy in copies:
        copy.start()
    copies[0].wait()
    inv[...] = lax.rsqrt(degree[...].astype(jnp.float32))
    for copy, half in zip(copies[1:], halves):
        copy.wait()
        scaled[half, :] = (features[half, :].astype(jnp.float32) * inv[...]).astype(scaled.dtype)


def backward_kernel(slot_ref, inv, weight_hbm, *refs, offsets, together):
    cots, refs = refs[: len(offsets)], refs[len(offsets) :]
    tiles_hbm, own_grad, pair_grad, diag_grad, acc, cot, weight, near, tiles, sems, in_sems, out_sems = refs
    blocks, slots, side, _ = tiles.shape
    width, nodes = own_grad.shape
    col = lax.axis_index("col")
    arrivals = [pltpu.make_async_copy(weight_hbm.at[block_at(col, width)], weight, in_sems.at[0])]
    for k, (value, offset) in enumerate(zip(cots, offsets)):
        place = cot.at[block_at(col ^ offset, width)]
        arrivals.append(pltpu.make_async_copy(value, place, in_sems.at[k + 1]))
    for copy in arrivals:
        copy.start()
    start_tiles(tiles_hbm, tiles, sems, 0, blocks)
    acc[...] = jnp.zeros_like(acc)
    for copy in arrivals:
        copy.wait()
    def mixed(first):
        here = pl.ds(pl.multiple_of(first * side, together * side), together * side)
        grad = jnp.dot(weight[...], cot[:, here], preferred_element_type=jnp.float32)
        return (grad * inv[:, here]).astype(cot.dtype)

    def block(b, grad):
        places = [block_at(slot_ref[b, s], side) for s in range(slots)]
        sums = [acc[:, place] for place in places]
        for group in slot_groups(slots):
            edges = jnp.concatenate([tiles[b, s] for s in group], axis=1)
            spread = jnp.dot(grad, edges, preferred_element_type=jnp.float32)
            for k, s in enumerate(group):
                acc[:, places[s]] = sums[s] + spread[:, k * side : (k + 1) * side]

    each_block(block, tiles_hbm, tiles, sems, together, mixed)
    own_copy = pltpu.make_async_copy(acc.at[:, :nodes], own_grad, out_sems.at[0])
    own_copy.start()
    near[...] = acc[:, nodes : 2 * nodes].astype(near.dtype)
    near_copy = pltpu.make_async_copy(near, pair_grad, out_sems.at[1])
    near_copy.start()
    diag_grad[...] = acc[:, 2 * nodes : 3 * nodes].astype(diag_grad.dtype)
    own_copy.wait()
    near_copy.wait()


def forward_kernel(slot_ref, inv, own, pair, diag, tiles_hbm, agg, window, tiles, sems, in_sems, *, together):
    blocks, slots, side, _ = tiles.shape
    width, nodes = agg.shape
    arrivals = [
        pltpu.make_async_copy(value, window.at[:, k * nodes : (k + 1) * nodes], in_sems.at[k])
        for k, value in enumerate((own, pair, diag))
    ]
    for copy in arrivals:
        copy.start()
    start_tiles(tiles_hbm, tiles, sems, 0, together)
    window[:, 3 * nodes :] = jnp.zeros((width, side), window.dtype)
    for copy in arrivals:
        copy.wait()
    start_tiles(tiles_hbm, tiles, sems, together, blocks)

    def block(b):
        places = [block_at(slot_ref[b, s], side) for s in range(slots)]
        total = None
        for group in slot_groups(slots):
            source = jnp.concatenate([window[:, places[s]] for s in group], axis=1)
            edges = jnp.concatenate([tiles[b, s] for s in group], axis=1)
            part = lax.dot_general(source, edges, CONTRACT_LAST, preferred_element_type=jnp.float32)
            total = part if total is None else total + part
        here = block_at(b, side)
        agg[:, here] = (total * inv[:, here]).astype(agg.dtype)

    each_block(block, tiles_hbm, tiles, sems, together)


def outer_kernel(*refs):
    cots, agg, out = refs[:-2], refs[-2], refs[-1]
    out[...] = jnp.concatenate(
        [
            lax.dot_general(c[...], agg[...], CONTRACT_LAST, preferred_element_type=jnp.float32)
            for c in cots
        ],
        axis=1,
    )


def shards(features, weight, cotangent, degree, tile_src, tile_count, tile_vals):
    width, nodes = features.shape
    blocks, slots, side, _ = tile_vals.shape
    rows = lax.axis_size("row")
    cols = lax.axis_size("col")
    row = lax.axis_index("row")
    col = lax.axis_index("col")
    offsets = pair_offsets(cols)
    vmem = pl.BlockSpec(memory_space=pltpu.VMEM)
    smem = pl.BlockSpec(memory_space=pltpu.SMEM)
    hbm = pl.BlockSpec(memory_space=pl.ANY)
    params = pltpu.CompilerParams(vmem_limit_bytes=VMEM_BYTES)
    light = pl.CostEstimate(flops=1, bytes_accessed=1, transcendentals=0)
    narrow = jax.ShapeDtypeStruct((width, nodes), jnp.bfloat16)
    full = jax.ShapeDtypeStruct((width, nodes), jnp.float32)
    together = math.gcd(blocks, 8)
    tile_scratch = [
        pltpu.VMEM(tile_vals.shape, tile_vals.dtype),
        pltpu.SemaphoreType.DMA((blocks,)),
    ]
    pairs = xor_pairs(rows, 1)
    outward = across(rows, 2)
    inward = [(target, source) for source, target in outward]

    scaled, inv_root = pl.pallas_call(
        scale_kernel,
        out_shape=(narrow, jax.ShapeDtypeStruct((1, nodes), jnp.float32)),
        in_specs=[hbm, hbm],
        out_specs=(vmem, vmem),
        scratch_shapes=[
            pltpu.VMEM((1, nodes), degree.dtype),
            pltpu.VMEM((width, nodes), features.dtype),
            pltpu.SemaphoreType.DMA((3,)),
        ],
        compiler_params=pltpu.CompilerParams(vmem_limit_bytes=VMEM_BYTES // 8),
        cost_estimate=light,
        name="scale",
    )(far(degree[None, :]), far(features))
    pair_scaled = lax.ppermute(scaled, "row", pairs)
    diag_scaled = lax.ppermute(pair_scaled, "row", outward)
    source_row = tile_src // blocks
    group = jnp.where(source_row == row, 0, jnp.where(source_row == (row ^ 1), 1, 2))
    live = jnp.arange(slots, dtype=jnp.int32)[None, :] < tile_count[:, None]
    slot_at = jnp.where(live, group * blocks + tile_src % blocks, 3 * blocks)
    cots = gather_pieces(cotangent, "col", (slot_at,))
    weight_cols = lax.dynamic_slice_in_dim(weight, col * width, width, 1)

    cots_here = tied(cots[1:], (pair_scaled,))
    own_grad, pair_grad, diag_grad = pl.pallas_call(
        functools.partial(backward_kernel, offsets=offsets, together=together),
        out_shape=(
            pltpu.HBM(full.shape, full.dtype),
            pltpu.HBM(narrow.shape, narrow.dtype),
            narrow,
        ),
        in_specs=[smem, vmem] + [hbm] * (cols + 2),
        out_specs=(hbm, hbm, vmem),
        scratch_shapes=[
            pltpu.VMEM((width, 3 * nodes + side), jnp.float32),
            pltpu.VMEM((width * cols, nodes), jnp.bfloat16),
            pltpu.VMEM((width, width * cols), jnp.bfloat16),
            pltpu.VMEM((width, nodes), jnp.bfloat16),
        ]
        + tile_scratch
        + [pltpu.SemaphoreType.DMA((cols + 1,)), pltpu.SemaphoreType.DMA((2,))],
        compiler_params=params,
        cost_estimate=light,
        name="backward_tiles",
    )(slot_at, inv_root, far(weight), far(cotangent), *cots_here, far(tile_vals))

    halos = tied((scaled, pair_scaled, diag_scaled), (diag_grad,))
    aggregated = pl.pallas_call(
        functools.partial(forward_kernel, together=together),
        out_shape=narrow,
        in_specs=[smem, vmem] + [hbm] * 4,
        out_specs=vmem,
        scratch_shapes=[pltpu.VMEM((width, 3 * nodes + side), jnp.bfloat16)]
        + tile_scratch
        + [pltpu.SemaphoreType.DMA((3,))],
        compiler_params=params,
        cost_estimate=light,
        name="forward_tiles",
    )(slot_at, inv_root, *halos, far(tile_vals))

    relayed = lax.ppermute(diag_grad, "row", inward)
    (relayed,) = tied((relayed,), (aggregated,))
    joined = (pair_grad.astype(jnp.float32) + relayed.astype(jnp.float32)).astype(jnp.bfloat16)
    returned = lax.ppermute(joined, "row", pairs)
    input_grad = (own_grad + returned.astype(jnp.float32)) * inv_root

    agg_pieces = gather_pieces(aggregated, "col")
    weight_parts = jnp.stack(
        [lax.dynamic_slice_in_dim(weight_cols, (col ^ o) * width, width, 0) for o in offsets]
    )
    output = lax.dot_general(
        weight_parts.reshape(cols * width, width),
        jnp.concatenate(agg_pieces, axis=0),
        (((0,), (0,)), ((), ())),
        preferred_element_type=jnp.float32,
    ).astype(jnp.bfloat16)

    outer = pl.pallas_call(
        outer_kernel,
        out_shape=jax.ShapeDtypeStruct((width, cols * width), jnp.float32),
        in_specs=[vmem] * (cols + 1),
        out_specs=vmem,
        compiler_params=pltpu.CompilerParams(vmem_limit_bytes=VMEM_BYTES // 4),
        cost_estimate=pl.CostEstimate(flops=1000000000, bytes_accessed=1, transcendentals=0),
        name="outer_product",
    )(*cots, aggregated)
    row_bits = bits_of(rows) if rows & (rows - 1) == 0 else []
    if not row_bits:
        outer = lax.psum(outer, "row")

    def over_rows(value, bits, after):
        for bit, others in zip(bits, after):
            if others:
                (value,) = tied((value,), others)
            value = value + lax.ppermute(value, "row", xor_pairs(rows, bit))
        return value

    known = [0]
    outer = over_rows(outer, row_bits[-1:], [()] * len(row_bits))
    blocks_of = {o: outer[:, k * width : (k + 1) * width] for k, o in enumerate(offsets)}
    for bit in reversed(bits_of(cols)):
        kept = [o for o in blocks_of if not o & bit]
        both = jnp.stack([blocks_of[o] for o in kept] + [blocks_of[o | bit] for o in kept])
        if 2 * bit == cols:
            both = over_rows(both, row_bits[:-1], [(joined,)] + [()] * len(row_bits))
            (both,) = tied((both,), (returned,))
        other = lax.ppermute(both[len(kept) :], "col", xor_pairs(cols, bit))
        blocks_of = {
            o: jnp.concatenate([both[k], other[k]], axis=1) for k, o in enumerate(kept)
        }
        known = known + [o ^ bit for o in known]
    total = blocks_of[0]
    place = jnp.asarray([known.index(o) for o in range(cols)], jnp.int32)
    weight_grad = jnp.concatenate(
        [
            lax.dynamic_slice_in_dim(total, place[col ^ c] * width, width, 1)
            for c in range(cols)
        ],
        axis=1,
    ) / math.sqrt(nodes * rows)
    return (output, input_grad, weight_grad.T)


def solution(mesh):
    placed = (
        P("col", "row"),
        P(),
        P("col", "row"),
        P("row"),
        P("row", None),
        P("row"),
        P("row", None, None, None),
    )
    return jax.shard_map(
        shards,
        mesh=mesh,
        in_specs=placed,
        out_specs=(P("col", "row"), P("col", "row"), P(None, "col")),
        check_vma=False,
    )
```
